512 devices in a mesh: seq: 16 (over x, y_hi, core), vocab: 32 (over y_lo, z).
Axes of the slice: x: 4, y: 8 (y_hi: 2, y_lo: 4; y = y_hi * 4 + y_lo), z: 8, core: 2. Of those that a mesh axis runs over, the one named last changes fastest.
Arguments:
- hidden_states: bfloat16 [384, 2304], P('seq', 'vocab'), may hold values from -6 to 6
- loss_mask: int32 [384], P('seq'), may hold values from 0 to 1, as said below
- teacher_probs: bfloat16 [384, 262144], P('seq', 'vocab'), may hold values from 1.899898e-07 to 1.9073486e-05
- head_weight: bfloat16 [2304, 32, 16, 512], P(None, 'vocab', 'seq'), may hold values from -0.5 to 0.5
Outputs:
- grad_hidden: bfloat16 [384, 2304], P('seq', 'vocab')
- grad_head: bfloat16 [2304, 32, 16, 512], P(None, 'vocab', 'seq')
The draws below stay inside these ranges and needn't reach their ends.
Inputs may be any that keep to these rules, and one draw needn't show every extreme that they name: `loss_mask`: the last token of the group always counts.
All inputs are finite; a program needn't handle non-finite values.
Results may differ from the reference program's by a relative error of at most 0.0049.
Values may be sent and summed in bfloat16 or wider, within the bound.
No kernel may reach another device: no remote copies, remote signals or barrier semaphores. Data moves between devices by JAX's collectives and lax.ppermute only.
A program may use at most 64 MiB of HBM per device.

```python
import math
import jax
import jax.numpy as jnp
from jax import lax

D = 2304
V_DEV = 512
TOKENS = 384
VOCAB = 262144
N_SEQ = 16
N_VOCAB = 32


def draw_loss_mask(key, part):
    key = jax.random.fold_in(key, 11)
    positions = jnp.arange(TOKENS, dtype=jnp.int32)
    limits = 250 + 700 * positions // TOKENS
    values = jax.random.randint(key, (TOKENS,), 0, 1000, dtype=jnp.int32)
    marked = jnp.where(values < limits, 1, 0).astype(jnp.int32)
    return jnp.where(positions == TOKENS - 1, 1, marked).astype(jnp.int32)


def draw_head_weight(key, part):
    key = jax.random.fold_in(key, 23)
    scale_key, base_key = jax.random.split(key)
    shape = (D, N_VOCAB, N_SEQ, V_DEV)
    column_scale = jnp.exp(jax.random.uniform(scale_key, (1, N_VOCAB, N_SEQ, V_DEV), jnp.float32, math.log(0.3), math.log(3.0)))
    base = jnp.clip(jax.random.normal(base_key, shape, jnp.float32), -6.0, 6.0)
    return (base * column_scale * D ** (-0.5)).astype(jnp.bfloat16)


def level_of(stream_key, dims, shards, low, top_value):
    def one(axis_at, blocks):
        steps = jax.random.uniform(jax.random.fold_in(jax.random.fold_in(stream_key, 6), axis_at), (blocks,), jnp.float32, low / len(shards), top_value / len(shards))
        return jnp.repeat(jnp.exp(steps), dims[axis_at] // blocks).reshape((-1,) + (1,) * (len(dims) - axis_at - 1))

    gain = one(*shards[0])
    for cut in shards[1:]:
        gain = gain * one(*cut)
    return gain


def noise(own_key, extent, deviation, reach, cuts=(), held_as=jnp.bfloat16):
    array = deviation * jax.random.normal(own_key, extent, jnp.float32)
    if cuts:
        array = array * level_of(own_key, extent, cuts, -0.22, 0.18)
    return jnp.clip(array, -reach, reach).astype(held_as)


def setup_inputs(seed: int = 0) -> dict:
    key_of = jax.random.split(jax.random.key(seed), 5)
    return {
        "hidden_states": noise(key_of[0], (TOKENS, D), 1.0, 6.0, ((0, 16), (1, 32))),
        "loss_mask": draw_loss_mask(jax.random.fold_in(key_of[4], 71), 0),
        "teacher_probs": jnp.clip(jnp.exp(math.log(1.9073486328125e-05) - 4.609084 * jax.random.uniform(key_of[2], (TOKENS, VOCAB), jnp.float32) ** level_of(key_of[2], (TOKENS, VOCAB), ((0, 16), (1, 32)), -0.2, 0.2)), 1.8998980522155762e-07, 1.9073486328125e-05).astype(jnp.bfloat16),
        "head_weight": draw_head_weight(jax.random.fold_in(key_of[4], 71), 0),
    }


def reference(hidden_states, loss_mask, teacher_probs, head_weight):
    columns = N_SEQ * V_DEV
    teacher_blocks = teacher_probs.reshape(TOKENS, N_VOCAB, columns)
    indices = jnp.arange(N_VOCAB, dtype=jnp.int32)

    def block_weight(index):
        return lax.dynamic_index_in_dim(head_weight, index, 1, keepdims=False).reshape(D, columns)

    def block_probs(index):
        return lax.dynamic_index_in_dim(teacher_blocks, index, 1, keepdims=False).astype(jnp.float32)

    def block_logits(index):
        raw_logits = jnp.dot(hidden_states, block_weight(index), preferred_element_type=jnp.float32)
        capped_tanh = jnp.tanh(raw_logits / 30.0)
        return capped_tanh, jnp.exp(30.0 * capped_tanh)

    def add_sums(carry, index):
        capped_tanh, exp_logits = block_logits(index)
        return (carry[0] + jnp.sum(exp_logits, axis=1), carry[1] + jnp.sum(block_probs(index), axis=1)), None

    zeros_row = jnp.zeros((TOKENS,), jnp.float32)
    (sum_exp, mass), unused = lax.scan(add_sums, (zeros_row, zeros_row), indices)
    weights_row = loss_mask.astype(jnp.float32)
    factor = 8.0 * VOCAB / jnp.sum(weights_row)

    def add_grads(carry, index):
        grad_sum, head_buffer = carry
        capped_tanh, exp_logits = block_logits(index)
        target = block_probs(index)
        grad_logits = (factor * weights_row[:, None] * (exp_logits / sum_exp[:, None] * mass[:, None] - target) * (1.0 - capped_tanh * capped_tanh)).astype(jnp.bfloat16)
        weight = block_weight(index)
        grad_sum = grad_sum + lax.dot_general(grad_logits, weight, (((1,), (1,)), ((), ())), preferred_element_type=jnp.float32)
        head_block = lax.dot_general(hidden_states, grad_logits, (((0,), (0,)), ((), ())), preferred_element_type=jnp.float32).astype(jnp.bfloat16)
        head_buffer = lax.dynamic_update_index_in_dim(head_buffer, head_block.reshape(D, N_SEQ, V_DEV), index, 1)
        return (grad_sum, head_buffer), None

    start_carry = (jnp.zeros((TOKENS, D), jnp.float32), jnp.zeros((D, N_VOCAB, N_SEQ, V_DEV), jnp.bfloat16))
    (grad_sum, grad_head), unused = lax.scan(add_grads, start_carry, indices)
    return grad_sum.astype(jnp.bfloat16), grad_head
```

```python
import jax
import jax.numpy as jnp
from jax import lax
from jax.experimental import pallas as pl
from jax.sharding import Mesh
from jax.sharding import PartitionSpec as P

SIZES = {"x": 4, "yh": 2, "c": 2, "yl": 4, "z": 8}
SEQ = ("x", "yh", "c")
VOCAB = ("yl", "z")
PLANE = ("yh", "yl", "z")
SWAP = [(0, 1), (1, 0)]
f32, bf16 = jnp.float32, jnp.bfloat16


def to_all(block, axes):
    count = 1
    for axis in axes:
        count *= SIZES[axis]
    return lax.all_to_all(
        jnp.broadcast_to(block[None], (count,) + block.shape), axes, 0, 0, tiled=True
    )


def softcap(rows, weight):
    capped_tanh = jnp.tanh(jnp.dot(rows, weight, preferred_element_type=f32) / 30.0)
    return capped_tanh, jnp.exp(30.0 * capped_tanh), 1.0 - capped_tanh * capped_tanh


def terms(exp_logits, target, slope, weight):
    both = jnp.concatenate([exp_logits * slope, target * slope])
    high = both.astype(bf16)
    low = (both - high.astype(f32)).astype(bf16)
    dims = (((1,), (1,)), ((), ()))
    return lax.dot_general(high, weight, dims, preferred_element_type=f32) + lax.dot_general(
        low, weight, dims, preferred_element_type=f32
    )


def packed(block):
    first, second, third = block[:8], block[8:16], block[16:]
    top = jnp.concatenate([first, second[:, :56]], axis=1)
    rest = jnp.concatenate([second[:, 56:], third, jnp.zeros((8, 40), block.dtype)], axis=1)
    return jnp.concatenate([top, rest], axis=0)


def unpacked(block):
    top, rest = block[..., :8, :], block[..., 8:, :]
    second = jnp.concatenate([top[..., 72:], rest[..., :16]], axis=-1)
    return jnp.concatenate([top[..., :72], second, rest[..., 16:88]], axis=-2)


def pack_copies_kernel(block_ref, out_ref):
    block = packed(block_ref[...].astype(f32)).astype(bf16)
    out_ref[...] = jnp.broadcast_to(block[None], out_ref.shape)


def pack_copies(block):
    out = jax.ShapeDtypeStruct((64, 16, 128), bf16)
    return pl.pallas_call(pack_copies_kernel, out_shape=out)(block)


def sum_pack_kernel(parts_ref, out_ref):
    for y_at in range(2):
        rows = pl.ds(24 * y_at, 24)
        total = parts_ref[0, rows, :].astype(f32)
        for x_at in range(1, 4):
            total = total + parts_ref[x_at, rows, :].astype(f32)
        for shard in range(32):
            out_ref[32 * y_at + shard] = packed(total[:, 72 * shard : 72 * shard + 72]).astype(bf16)


def sum_pack(parts):
    out = jax.ShapeDtypeStruct((64, 16, 128), bf16)
    return pl.pallas_call(sum_pack_kernel, out_shape=out)(parts)


def sum_unpack_kernel(parts_ref, out_ref):
    total = parts_ref[0].astype(f32)
    for at in range(1, 64):
        total = total + parts_ref[at].astype(f32)
    out_ref[...] = unpacked(total).astype(bf16)


def sum_unpack(parts):
    out = jax.ShapeDtypeStruct((24, 72), bf16)
    return pl.pallas_call(sum_unpack_kernel, out_shape=out)(parts)


def shards(hidden_states, loss_mask, teacher_probs, head_weight):
    tokens, features = hidden_states.shape
    feature_dim, shard_cols = head_weight.shape[0], head_weight.shape[3]
    half = 8 * tokens
    weight = head_weight.reshape(feature_dim, shard_cols)
    y_at, core = lax.axis_index("yh"), lax.axis_index("c")

    plane = unpacked(lax.all_to_all(pack_copies(hidden_states), PLANE, 0, 0, tiled=True))
    plane = plane.reshape(2, 32, tokens, features)
    rows = plane.transpose(0, 2, 1, 3).reshape(2 * tokens, feature_dim)

    by_owner = teacher_probs.reshape(tokens, 4, 2, 2, shard_cols)

    def piece(other_y, other_core):
        start = (0, 0, y_at ^ other_y, core ^ other_core, 0)
        block = lax.dynamic_slice(by_owner, start, (tokens, 4, 1, 1, shard_cols))
        block = block.reshape(tokens, 4, shard_cols).transpose(1, 0, 2)
        if not (other_y or other_core):
            return block
        step = 2 * other_y + other_core
        return lax.ppermute(block, ("yh", "c"), [(i, i ^ step) for i in range(4)])

    def both_y(other_core):
        near, far = piece(0, other_core), piece(1, other_core)
        low, high = jnp.where(y_at == 0, near, far), jnp.where(y_at == 0, far, near)
        return jnp.concatenate([low, high], axis=1)

    mass_part = jnp.sum(teacher_probs.astype(f32), axis=1)

    sent = jnp.concatenate(
        [jnp.broadcast_to(rows[None], (4,) + rows.shape), both_y(0), both_y(1)], axis=2
    )
    got = lax.all_to_all(sent, "x", 0, 0, tiled=True).reshape(half, feature_dim + 2 * shard_cols)
    mine = got[:, :feature_dim]
    other = lax.ppermute(mine, "c", SWAP)
    target_mine = got[:, feature_dim : feature_dim + shard_cols].astype(f32)
    target_other = got[:, feature_dim + shard_cols :].astype(f32)

    tanh_mine, exp_mine, slope_mine = softcap(mine, weight)
    tanh_other, exp_other, slope_other = softcap(other, weight)

    stats = jnp.concatenate(
        [
            jnp.sum(exp_mine, axis=1),
            jnp.sum(exp_other, axis=1),
            mass_part,
            jnp.zeros((128 - tokens,), f32),
        ]
    ).reshape(4, 128)
    stats = jnp.sum(to_all(stats, VOCAB), axis=0)
    masks = jnp.concatenate(
        [jnp.zeros((tokens,), f32), loss_mask.astype(f32), jnp.zeros((128 - 2 * tokens,), f32)]
    )
    stats = jnp.concatenate([stats[:3], stats[3:] + masks[None]])
    stats, terms_mine, terms_other = lax.optimization_barrier(
        (
            stats,
            terms(exp_mine, target_mine, slope_mine, weight),
            terms(exp_other, target_other, slope_other, weight),
        )
    )
    stats = to_all(stats, SEQ)
    sums = jnp.sum(stats[:, :3].reshape(8, 2, 2, half), axis=0)
    sum_mine = jnp.where(core == 0, sums[0, 0] + sums[1, 1], sums[1, 0] + sums[0, 1])
    sum_other = jnp.where(core == 0, sums[0, 1] + sums[1, 0], sums[1, 1] + sums[0, 0])

    def by_core(values):
        values = values.reshape(8, 2, tokens)
        zero, one = values[:, 0].reshape(half), values[:, 1].reshape(half)
        return jnp.where(core == 0, zero, one), jnp.where(core == 0, one, zero)

    mass_mine, mass_other = by_core(stats[:, 3, :tokens])
    mask_mine, mask_other = by_core(stats[:, 3, tokens : 2 * tokens])
    both = terms_mine + lax.ppermute(terms_other, "c", SWAP)

    masked_count = jnp.sum(mask_mine) + jnp.sum(mask_other)
    factor = 8.0 * (shard_cols * 512) / masked_count

    def logit_grad(sum_exp, mass, mask, exp_logits, target, slope):
        return (
            factor
            * mask[:, None]
            * (exp_logits / sum_exp[:, None] * mass[:, None] - target)
            * slope
        ).astype(bf16)

    grad_logits = jnp.concatenate(
        [
            logit_grad(sum_mine, mass_mine, mask_mine, exp_mine, target_mine, slope_mine),
            logit_grad(sum_other, mass_other, mask_other, exp_other, target_other, slope_other),
        ]
    )
    states = jnp.concatenate([mine, other])
    head_grad = lax.dot_general(
        states, grad_logits, (((0,), (0,)), ((), ())), preferred_element_type=f32
    )
    grad_head = head_grad.astype(bf16).reshape(head_weight.shape)

    ratio = (mass_mine / sum_mine)[:, None]
    part = (factor * mask_mine)[:, None] * (both[:half] * ratio - both[half:])
    part = part.astype(bf16).reshape(4, 2 * tokens, feature_dim)
    part = sum_pack(lax.all_to_all(part, "x", 0, 0, tiled=True))
    grad_hidden = sum_unpack(lax.all_to_all(part, PLANE, 0, 0, tiled=True))
    return grad_hidden, grad_head


def solution(mesh):
    fine = Mesh(mesh.devices.reshape(tuple(SIZES.values())), tuple(SIZES))
    head = P(None, VOCAB, SEQ, None)
    return jax.shard_map(
        shards,
        mesh=fine,
        in_specs=(P(SEQ, VOCAB), P(SEQ), P(SEQ, VOCAB), head),
        out_specs=(P(SEQ, VOCAB), head),
        check_vma=False,
    )
```

```python
import jax
import jax.numpy as jnp
from jax import lax
from jax.experimental import pallas as pl
from jax.experimental.pallas import tpu as pltpu
from jax.sharding import Mesh
from jax.sharding import PartitionSpec as P

SIZES = {"x": 4, "yh": 2, "c": 2, "yl": 4, "z": 8}
SEQ = ("x", "yh", "c")
VOCAB = ("yl", "z")
PLANE = ("yh", "yl", "z")
SWAP = [(0, 1), (1, 0)]
f32, bf16 = jnp.float32, jnp.bfloat16


KERNEL = pltpu.CompilerParams(vmem_limit_bytes=24 * 1024 * 1024)
IN_HBM = pl.BlockSpec(memory_space=pltpu.HBM)
IN_VMEM = pl.BlockSpec(memory_space=pltpu.VMEM)
HELD = (4, 2304, 256)


def in_hbm(array):
    return pltpu.with_memory_space_constraint(array, pltpu.HBM)


def logits_kernel(
    got_ref, own_ref, far_ref, extra_ref, exp_ref, slope_ref, stats_ref, give_ref, held, sems
):
    copies = []
    for at in range(4):
        source = (own_ref, far_ref)[at // 2].at[:, pl.ds(256 * (at % 2), 256)]
        copies.append(pltpu.make_async_copy(source, held.at[at], sems.at[at]))
        copies[at].start()
    depth = own_ref.shape[0]
    rows = jnp.concatenate([got_ref[at, :, :depth] for at in range(4)], axis=0)
    for at in range(4):
        give_ref[at] = got_ref[at, :, depth:].astype(f32)[24:].astype(bf16)
    sums = jnp.zeros((192, 1), f32)
    for at in range(4):
        copies[at].wait()
        logits = jnp.dot(rows, held[at], preferred_element_type=f32)
        capped_tanh = jnp.tanh(logits / 30.0)
        exp_logits = jnp.exp(30.0 * capped_tanh)
        columns = slice(256 * at, 256 * at + 256)
        exp_ref[:, columns] = exp_logits
        slope_ref[:, columns] = 1.0 - capped_tanh * capped_tanh
        sums = sums + jnp.sum(exp_logits, axis=1, keepdims=True)
    wide = jnp.broadcast_to(sums, (192, 128))
    first = jnp.transpose(wide[:128])[:1]
    last = jnp.transpose(jnp.concatenate([wide[128:], jnp.zeros((64, 128), f32)], axis=0))[:1]
    lane = lax.broadcasted_iota(jnp.int32, (1, 128), 1)
    stats = jnp.concatenate([first, jnp.where(lane < 64, last, extra_ref[...])], axis=0)
    stats_ref[...] = jnp.broadcast_to(stats[None], stats_ref.shape)


def logits_of(got, own, far, extra):
    wide = jax.ShapeDtypeStruct((192, 1024), f32)
    stats = jax.ShapeDtypeStruct((64, 2, 128), f32)
    return pl.pallas_call(
        logits_kernel,
        in_specs=[IN_VMEM, IN_HBM, IN_HBM, IN_VMEM],
        out_shape=(wide, wide, stats, jax.ShapeDtypeStruct((4, 24, 1024), bf16)),
        scratch_shapes=[pltpu.VMEM(HELD, bf16), pltpu.SemaphoreType.DMA((4,))],
        compiler_params=KERNEL,
    )(got, in_hbm(own), in_hbm(far), extra)


def stats_kernel(stats_ref, out_ref):
    first = stats_ref[0, :1, :]
    for at in range(1, 64):
        first = first + stats_ref[at, :1, :]
    halves = []
    for y_at in range(2):
        total = stats_ref[32 * y_at, 1:, :]
        for at in range(1, 32):
            total = total + stats_ref[32 * y_at + at, 1:, :]
        halves.append(total)
    lane = lax.broadcasted_iota(jnp.int32, (1, 128), 1)
    low = jnp.where(lane < 88, halves[0], stats_ref[0, 1:, :])
    high = jnp.where(lane < 88, halves[1], stats_ref[32, 1:, :])
    low = jnp.where(lane < 64, halves[0] + halves[1], low)
    rows = jnp.concatenate([first, low, high, high], axis=0)
    out_ref[...] = jnp.broadcast_to(rows[None], out_ref.shape)


def stats_over_plane(stats):
    out = jax.ShapeDtypeStruct((4, 4, 128), f32)
    return pl.pallas_call(stats_kernel, out_shape=out)(stats)


def grads_kernel(
    stats_ref,
    exp_ref,
    slope_ref,
    target_ref,
    own_ref,
    far_ref,
    part_ref,
    grad_own_ref,
    grad_far_ref,
    held,
    made,
    sems,
    out_sems,
):
    copies = []
    for at in range(4):
        source = (own_ref, far_ref)[at % 2].at[pl.ds(1152 * (at // 2), 1152), :]
        copies.append(pltpu.make_async_copy(source, held.at[at], sems.at[at]))
        copies[at].start()
    firsts = [stats_ref[at, :1, :] for at in range(4)]
    seconds = [stats_ref[at // 2, 1 + at % 2 : 2 + at % 2, :] for at in range(8)]
    rows = jnp.concatenate([sum(firsts), sum(seconds[::2])] + seconds, axis=0)
    lane = lax.broadcasted_iota(jnp.int32, (1, 128), 1)
    counted = jnp.where((lane >= 88) & (lane < 113), sum(seconds), 0.0)
    factor = 8.0 * 262144 / jnp.sum(counted, axis=1, keepdims=True)
    columns = jnp.transpose(jnp.concatenate([rows, jnp.zeros((118, 128), f32)], axis=0))
    sum_exp = jnp.concatenate([columns[:, 0:1], columns[:64, 1:2]], axis=0)
    mass = jnp.concatenate([columns[64:88, 2 + at : 3 + at] for at in range(8)], axis=0)
    mask = jnp.concatenate([columns[88:112, 2 + at : 3 + at] for at in range(8)], axis=0)
    scale, share = factor * mask, mass / sum_exp
    grads = []
    for half_at, grad_ref in enumerate((grad_own_ref, grad_far_ref)):
        entries = slice(512 * half_at, 512 * half_at + 512)
        grad = scale * (exp_ref[:, entries] * share - target_ref[:, entries].astype(f32))
        grad = (grad * slope_ref[:, entries]).astype(bf16)
        grad_ref[...] = grad
        grads.append(grad)
    dims = (((1,), (1,)), ((), ()))
    sent = []
    for half_at in range(2):
        copies[2 * half_at].wait()
        copies[2 * half_at + 1].wait()
        for start in range(0, 1152, 384):
            block = slice(start, start + 384)
            part = lax.dot_general(
                grads[0], held[2 * half_at, block, :], dims, preferred_element_type=f32
            ) + lax.dot_general(
                grads[1], held[2 * half_at + 1, block, :], dims, preferred_element_type=f32
            )
            part = part.astype(bf16)
            for at in range(4):
                made[half_at, at, :, block] = part[48 * at : 48 * at + 48]
        target = part_ref.at[:, :, pl.ds(1152 * half_at, 1152)]
        sent.append(pltpu.make_async_copy(made.at[half_at], target, out_sems.at[half_at]))
        sent[half_at].start()
    for copy in sent:
        copy.wait()


def grads_of(stats, exp_logits, slope, target, own, far):
    grad = pltpu.HBM((192, 512), bf16)
    return pl.pallas_call(
        grads_kernel,
        in_specs=[IN_VMEM] * 4 + [IN_HBM] * 2,
        out_specs=(IN_HBM, IN_VMEM, IN_VMEM),
        out_shape=(pltpu.HBM((4, 48, own.shape[0]), bf16), grad, grad),
        scratch_shapes=[
            pltpu.VMEM((4, 1152, 512), bf16),
            pltpu.VMEM((2, 4, 48, 1152), bf16),
            pltpu.SemaphoreType.DMA((4,)),
            pltpu.SemaphoreType.DMA((2,)),
        ],
        compiler_params=KERNEL,
    )(stats, exp_logits, slope, target, in_hbm(own), in_hbm(far))


def packed(block):
    first, second, third = block[:8], block[8:16], block[16:]
    top = jnp.concatenate([first, second[:, :56]], axis=1)
    rest = jnp.concatenate([second[:, 56:], third, jnp.zeros((8, 40), block.dtype)], axis=1)
    return jnp.concatenate([top, rest], axis=0)


def unpacked(block):
    top, rest = block[..., :8, :], block[..., 8:, :]
    second = jnp.concatenate([top[..., 72:], rest[..., :16]], axis=-1)
    return jnp.concatenate([top[..., :72], second, rest[..., 16:88]], axis=-2)


def pack_copies_kernel(block_ref, out_ref):
    block = packed(block_ref[...].astype(f32)).astype(bf16)
    out_ref[...] = jnp.broadcast_to(block[None], out_ref.shape)


def pack_copies(block):
    out = jax.ShapeDtypeStruct((64, 16, 128), bf16)
    return pl.pallas_call(pack_copies_kernel, out_shape=out)(block)


def sum_pack_kernel(parts_ref, out_ref, held, sems):
    copies = []
    for at in range(2):
        source = parts_ref.at[:, :, pl.ds(1152 * at, 1152)]
        copies.append(pltpu.make_async_copy(source, held.at[at], sems.at[at]))
        copies[at].start()
    for at in range(2):
        copies[at].wait()
        total = held[at, 0].astype(f32)
        for x_at in range(1, 4):
            total = total + held[at, x_at].astype(f32)
        for shard in range(16):
            columns = total[:, 72 * shard : 72 * shard + 72]
            for y_at in range(2):
                block = packed(columns[24 * y_at : 24 * y_at + 24])
                out_ref[32 * y_at + 16 * at + shard] = block.astype(bf16)


def sum_pack(parts):
    return pl.pallas_call(
        sum_pack_kernel,
        in_specs=[IN_HBM],
        out_shape=jax.ShapeDtypeStruct((64, 16, 128), bf16),
        scratch_shapes=[pltpu.VMEM((2, 4, 48, 1152), bf16), pltpu.SemaphoreType.DMA((2,))],
        compiler_params=KERNEL,
    )(parts)


def shards(hidden_states, loss_mask, teacher_probs, head_weight):
    tokens, features = hidden_states.shape
    feature_dim, shard_cols = head_weight.shape[0], head_weight.shape[3]
    half = 8 * tokens
    weight = head_weight.reshape(feature_dim, shard_cols)
    y_at, core = lax.axis_index("yh"), lax.axis_index("c")

    copies, weight, teacher_probs, loss_mask = lax.optimization_barrier(
        (pack_copies(hidden_states), weight, teacher_probs, loss_mask)
    )
    plane = unpacked(lax.all_to_all(copies, PLANE, 0, 0, tiled=True))
    plane = plane.reshape(2, 32, tokens, features)
    rows = plane.transpose(0, 2, 1, 3).reshape(2 * tokens, feature_dim)

    weight_other = lax.ppermute(weight, "c", SWAP)
    mask_mine = loss_mask.astype(f32)
    mask_other = lax.ppermute(mask_mine, "c", SWAP)
    mass_part = jnp.sum(teacher_probs.astype(f32), axis=1)

    by_owner = teacher_probs.reshape(tokens, 4, 2, 2, shard_cols)


    def entries(far_y, far_core):
        at_zero, at_one = (
            jnp.where((core == 0) != far_core, by_owner[:, :, at, 0], by_owner[:, :, at, 1])
            for at in range(2)
        )
        return jnp.where((y_at == 0) != far_y, at_zero, at_one).transpose(1, 0, 2)

    by_owner = jnp.concatenate(
        [
            jnp.concatenate([entries(far_y, far_core) for far_core in (False, True)], axis=2)
            for far_y in (False, True)
        ],
        axis=1,
    )

    blank = half - 128
    extra = jnp.concatenate(
        [
            jnp.zeros((blank,), f32),
            mass_part,
            mask_mine,
            jnp.sum(mask_other, keepdims=True),
            jnp.zeros((128 - blank - 2 * tokens - 1,), f32),
        ]
    )

    sent = jnp.concatenate([jnp.broadcast_to(rows[None], (4,) + rows.shape), by_owner], axis=2)
    sent, extra = lax.optimization_barrier((sent, extra))
    got = lax.all_to_all(sent, "x", 0, 0, tiled=True)

    exp_logits, slope, stats, give = logits_of(got, weight, weight_other, extra[None])
    stats = stats_over_plane(lax.all_to_all(stats, PLANE, 0, 0, tiled=True))
    stats = lax.all_to_all(stats, "x", 0, 0, tiled=True)

    kept, came = got[:, :tokens, feature_dim:], lax.ppermute(give, "yh", SWAP)
    low, high = jnp.where(y_at == 0, kept, came), jnp.where(y_at == 0, came, kept)
    target = jnp.stack([low, high], axis=1).reshape(half, 2 * shard_cols)

    stats, target = lax.optimization_barrier((stats, target))
    part, grad_own, grad_far = grads_of(stats, exp_logits, slope, target, weight, weight_other)
    mine = got[:, :, :feature_dim].reshape(half, feature_dim)

    states = jnp.concatenate([mine, lax.ppermute(mine, "c", SWAP)])
    grad_logits = jnp.concatenate([grad_own, lax.ppermute(grad_far, "c", SWAP)])
    head_grad = lax.dot_general(
        states, grad_logits, (((0,), (0,)), ((), ())), preferred_element_type=f32
    )
    grad_head = head_grad.astype(bf16).reshape(head_weight.shape)

    part = sum_pack(lax.all_to_all(part, "x", 0, 0, tiled=True))
    part = lax.all_to_all(part, PLANE, 0, 0, tiled=True)
    grad_hidden = unpacked(jnp.sum(part.astype(f32), axis=0)).astype(bf16)
    return grad_hidden, grad_head


def solution(mesh):
    fine = Mesh(mesh.devices.reshape(tuple(SIZES.values())), tuple(SIZES))
    head = P(None, VOCAB, SEQ, None)
    return jax.shard_map(
        shards,
        mesh=fine,
        in_specs=(P(SEQ, VOCAB), P(SEQ), P(SEQ, VOCAB), head),
        out_specs=(P(SEQ, VOCAB), head),
        check_vma=False,
    )
```

```python
import jax
import jax.numpy as jnp
from jax import lax
from jax.experimental import pallas as pl
from jax.experimental.pallas import tpu as pltpu
from jax.sharding import Mesh
from jax.sharding import PartitionSpec as P

SIZES = {"x": 4, "yh": 2, "c": 2, "yl": 4, "z": 8}
SEQ = ("x", "yh", "c")
VOCAB = ("yl", "z")
PLANE = ("yh", "yl", "z")
SWAP = [(0, 1), (1, 0)]
f32, bf16 = jnp.float32, jnp.bfloat16


KERNEL = pltpu.CompilerParams(vmem_limit_bytes=24 * 1024 * 1024)
IN_HBM = pl.BlockSpec(memory_space=pltpu.HBM)
IN_VMEM = pl.BlockSpec(memory_space=pltpu.VMEM)
HELD = (2, 2304, 256)


def in_hbm(array):
    return pltpu.with_memory_space_constraint(array, pltpu.HBM)


def logits_kernel(
    got_ref,
    own_ref,
    far_ref,
    mass_ref,
    mask_ref,
    far_mask_ref,
    tanh_ref,
    stats_ref,
    held,
    made,
    sems,
    out_sems,
):
    copies = []
    for at in range(2):
        source = far_ref.at[:, pl.ds(256 * at, 256)]
        copies.append(pltpu.make_async_copy(source, held.at[at], sems.at[at]))
        copies[at].start()
    rows = jnp.concatenate([got_ref[at] for at in range(4)], axis=0)
    sums, sent = jnp.zeros((192, 1), f32), []
    for at in range(4):
        columns = slice(256 * at, 256 * at + 256)
        if at >= 2:
            copies[at - 2].wait()
        weight = own_ref[:, columns] if at < 2 else held[at - 2]
        logits = jnp.dot(rows, weight, preferred_element_type=f32)
        capped_tanh = jnp.tanh(logits * (1.0 / 30.0))
        made[at] = capped_tanh
        target = tanh_ref.at[:, pl.ds(256 * at, 256)]
        sent.append(pltpu.make_async_copy(made.at[at], target, out_sems.at[at]))
        sent[at].start()
        sums = sums + jnp.sum(jnp.exp(30.0 * capped_tanh), axis=1, keepdims=True)
    wide = jnp.broadcast_to(sums, (192, 128))
    first = jnp.transpose(wide[:128])[:1]
    last = jnp.concatenate([wide[128:], mass_ref[...], jnp.zeros((40, 128), f32)], axis=0)
    last = jnp.transpose(last)[:1]
    count = jnp.sum(far_mask_ref[...], axis=1, keepdims=True)
    blank, rest = jnp.zeros((1, 88), f32), jnp.zeros((1, 15), f32)
    extra = jnp.concatenate([blank, mask_ref[...], count, rest], axis=1)
    lane = lax.broadcasted_iota(jnp.int32, (1, 128), 1)
    stats = jnp.concatenate([first, jnp.where(lane < 88, last, extra)], axis=0)
    stats_ref[...] = jnp.broadcast_to(stats[None], stats_ref.shape)
    for copy in sent:
        copy.wait()


def logits_of(got, own, far, mass, mask, far_mask):
    wide = pltpu.HBM((192, 1024), f32)
    stats = jax.ShapeDtypeStruct((64, 2, 128), f32)
    return pl.pallas_call(
        logits_kernel,
        in_specs=[IN_VMEM, IN_VMEM, IN_HBM] + [IN_VMEM] * 3,
        out_specs=(IN_HBM, IN_VMEM),
        out_shape=(wide, stats),
        scratch_shapes=[
            pltpu.VMEM(HELD, bf16),
            pltpu.VMEM((4, 192, 256), f32),
            pltpu.SemaphoreType.DMA((2,)),
            pltpu.SemaphoreType.DMA((4,)),
        ],
        compiler_params=KERNEL,
    )(got, own, in_hbm(far), mass, mask, far_mask)


def teacher_kernel(probs_ref, near_ref, give_ref, mass_ref):
    y_at, core = lax.axis_index("yh"), lax.axis_index("c")
    for x_at in range(4):
        for out_ref, y_of in ((near_ref, y_at), (give_ref, 1 - y_at)):
            for which, core_of in enumerate((core, 1 - core)):
                start = pl.multiple_of(2048 * x_at + 1024 * y_of + 512 * core_of, 512)
                out_ref[x_at, :, 512 * which : 512 * which + 512] = probs_ref[:, pl.ds(start, 512)]
    total = probs_ref[:, :128].astype(f32)
    for start in range(128, 8192, 128):
        total = total + probs_ref[:, start : start + 128].astype(f32)
    mass_ref[...] = jnp.broadcast_to(jnp.sum(total, axis=1, keepdims=True), (24, 128))


def teacher_parts(probs):
    part = jax.ShapeDtypeStruct((4, 24, 1024), bf16)
    out = (part, part, jax.ShapeDtypeStruct((24, 128), f32))
    return pl.pallas_call(teacher_kernel, out_shape=out, compiler_params=KERNEL)(probs)


def stats_kernel(stats_ref, target_ref, out_ref):
    first = stats_ref[0, :1, :]
    for at in range(1, 64):
        first = first + stats_ref[at, :1, :]
    halves = []
    for y_at in range(2):
        total = stats_ref[32 * y_at, 1:, :]
        for at in range(1, 32):
            total = total + stats_ref[32 * y_at + at, 1:, :]
        halves.append(total)
    lane = lax.broadcasted_iota(jnp.int32, (1, 128), 1)
    low = jnp.where(lane < 88, halves[0], stats_ref[0, 1:, :])
    high = jnp.where(lane < 88, halves[1], stats_ref[32, 1:, :])
    low = jnp.where(lane < 64, halves[0] + halves[1], low)
    rows = jnp.concatenate([first, low, high, high], axis=0)
    top = rows.astype(bf16).astype(f32)
    middle = (rows - top).astype(bf16).astype(f32)
    split = [top, middle, rows - top - middle, jnp.zeros((36, 128), f32)]
    split = jnp.concatenate(split, axis=0).astype(bf16)
    for at in range(4):
        out_ref[at, :, :1024] = target_ref[at]
        out_ref[at, :, 1024:] = split


def stats_over_plane(stats, target):
    out = jax.ShapeDtypeStruct((4, 48, 1152), bf16)
    return pl.pallas_call(stats_kernel, out_shape=out, compiler_params=KERNEL)(stats, target)


def grads_kernel(
    got_ref,
    tanh_ref,
    own_ref,
    far_ref,
    part_ref,
    grad_own_ref,
    grad_far_ref,
    held,
    made,
    grads,
    sems,
    out_sems,
    grad_sems,
):
    copies = []
    for at in range(6):
        source = (own_ref, far_ref)[at % 2].at[pl.ds(768 * (at // 2), 768), :]
        copies.append(pltpu.make_async_copy(source, held.at[at], sems.at[at]))
        copies[at].start()
    stats = []
    for at in range(4):
        split = got_ref[at, :, 1024:].astype(f32)
        stats.append(split[0:4] + split[4:8] + split[8:12])
    firsts = [stats[at][:1] for at in range(4)]
    seconds = [stats[at // 2][1 + at % 2 : 2 + at % 2] for at in range(8)]
    rows = jnp.concatenate([sum(firsts), sum(seconds[::2])] + seconds, axis=0)
    lane = lax.broadcasted_iota(jnp.int32, (1, 128), 1)
    counted = jnp.where((lane >= 88) & (lane < 113), sum(seconds), 0.0)
    factor = 8.0 * 262144 / jnp.sum(counted, axis=1, keepdims=True)
    columns = jnp.transpose(jnp.concatenate([rows, jnp.zeros((118, 128), f32)], axis=0))
    sum_exp = jnp.concatenate([columns[:, 0:1], columns[:64, 1:2]], axis=0)
    mass = jnp.concatenate([columns[64:88, 2 + at : 3 + at] for at in range(8)], axis=0)
    mask = jnp.concatenate([columns[88:112, 2 + at : 3 + at] for at in range(8)], axis=0)
    scale, share = factor * mask, mass / sum_exp
    sent = []
    for at, grad_ref in enumerate((grad_own_ref, grad_far_ref)):
        entries = slice(512 * at, 512 * at + 512)
        capped_tanh = tanh_ref[:, entries]
        target = jnp.concatenate([got_ref[x_at, :, entries].astype(f32) for x_at in range(4)])
        grad = jnp.exp(30.0 * capped_tanh) * share - target
        grads[at] = (scale * grad * (1.0 - capped_tanh * capped_tanh)).astype(bf16)
        sent.append(pltpu.make_async_copy(grads.at[at], grad_ref, grad_sems.at[at]))
        sent[at].start()
    dims = (((1,), (1,)), ((), ()))
    for at in range(3):
        copies[2 * at].wait()
        copies[2 * at + 1].wait()
        for start in (0, 384):
            inner = slice(start, start + 384)
            part = lax.dot_general(
                grads[0], held[2 * at, inner, :], dims, preferred_element_type=f32
            ) + lax.dot_general(
                grads[1], held[2 * at + 1, inner, :], dims, preferred_element_type=f32
            )
            part = part.astype(bf16)
            for x_at in range(4):
                made[at, x_at, :, inner] = part[48 * x_at : 48 * x_at + 48]
        target = part_ref.at[:, :, pl.ds(768 * at, 768)]
        sent.append(pltpu.make_async_copy(made.at[at], target, out_sems.at[at]))
        sent[2 + at].start()
    for copy in sent:
        copy.wait()


def grads_of(got, capped_tanh, own, far):
    grad = pltpu.HBM((192, 512), bf16)
    return pl.pallas_call(
        grads_kernel,
        in_specs=[IN_VMEM] * 2 + [IN_HBM] * 2,
        out_specs=(IN_HBM, IN_HBM, IN_HBM),
        out_shape=(pltpu.HBM((4, 48, own.shape[0]), bf16), grad, grad),
        scratch_shapes=[
            pltpu.VMEM((6, 768, 512), bf16),
            pltpu.VMEM((3, 4, 48, 768), bf16),
            pltpu.VMEM((2, 192, 512), bf16),
            pltpu.SemaphoreType.DMA((6,)),
            pltpu.SemaphoreType.DMA((3,)),
            pltpu.SemaphoreType.DMA((2,)),
        ],
        compiler_params=KERNEL,
    )(got, capped_tanh, in_hbm(own), in_hbm(far))


def packed(block):
    first, second, third = block[:8], block[8:16], block[16:]
    top = jnp.concatenate([first, second[:, :56]], axis=1)
    rest = jnp.concatenate([second[:, 56:], third, jnp.zeros((8, 40), block.dtype)], axis=1)
    return jnp.concatenate([top, rest], axis=0)


def unpacked(block):
    top, rest = block[..., :8, :], block[..., 8:, :]
    second = jnp.concatenate([top[..., 72:], rest[..., :16]], axis=-1)
    return jnp.concatenate([top[..., :72], second, rest[..., 16:88]], axis=-2)


def pack_copies_kernel(block_ref, out_ref):
    block = packed(block_ref[...].astype(f32)).astype(bf16)
    out_ref[...] = jnp.broadcast_to(block[None], out_ref.shape)


def pack_copies(block):
    out = jax.ShapeDtypeStruct((64, 16, 128), bf16)
    return pl.pallas_call(pack_copies_kernel, out_shape=out, compiler_params=KERNEL)(block)


def sum_pack_kernel(parts_ref, out_ref, held, sems):
    copies = []
    for at in range(2):
        source = parts_ref.at[:, :, pl.ds(1152 * at, 1152)]
        copies.append(pltpu.make_async_copy(source, held.at[at], sems.at[at]))
        copies[at].start()
    for at in range(2):
        copies[at].wait()
        total = held[at, 0].astype(f32)
        for x_at in range(1, 4):
            total = total + held[at, x_at].astype(f32)
        for shard in range(16):
            columns = total[:, 72 * shard : 72 * shard + 72]
            for y_at in range(2):
                block = packed(columns[24 * y_at : 24 * y_at + 24])
                out_ref[32 * y_at + 16 * at + shard] = block.astype(bf16)


def sum_pack(parts):
    return pl.pallas_call(
        sum_pack_kernel,
        in_specs=[IN_HBM],
        out_shape=jax.ShapeDtypeStruct((64, 16, 128), bf16),
        scratch_shapes=[pltpu.VMEM((2, 4, 48, 1152), bf16), pltpu.SemaphoreType.DMA((2,))],
        compiler_params=KERNEL,
    )(parts)


def shards(hidden_states, loss_mask, teacher_probs, head_weight):
    tokens, features = hidden_states.shape
    feature_dim, shard_cols = head_weight.shape[0], head_weight.shape[3]
    half = 8 * tokens
    weight = head_weight.reshape(feature_dim, shard_cols)
    y_at = lax.axis_index("yh")

    copies, weight, teacher_probs, loss_mask = lax.optimization_barrier(
        (pack_copies(hidden_states), weight, teacher_probs, loss_mask)
    )
    plane = unpacked(lax.all_to_all(copies, PLANE, 0, 0, tiled=True))
    plane = plane.reshape(2, 32, tokens, features)
    rows = plane.transpose(0, 2, 1, 3).reshape(2 * tokens, feature_dim)

    weight_other = lax.ppermute(weight, "c", SWAP)
    mask_mine = loss_mask.astype(f32)
    mask_other = lax.ppermute(mask_mine, "c", SWAP)

    near, give, mass_part = teacher_parts(teacher_probs)
    came = lax.ppermute(give, "yh", SWAP)

    rows, mask_other = lax.optimization_barrier((rows, mask_other))
    got = lax.all_gather(rows, "x", axis=0)
    got, came = lax.optimization_barrier((got, came))
    low, high = jnp.where(y_at == 0, near, came), jnp.where(y_at == 0, came, near)
    target = jnp.concatenate([low, high], axis=1)

    capped_tanh, stats = logits_of(
        got, weight, weight_other, mass_part, mask_mine[None], mask_other[None]
    )
    stats = stats_over_plane(lax.all_to_all(stats, PLANE, 0, 0, tiled=True), target)
    stats = lax.all_to_all(stats, "x", 0, 0, tiled=True)
    part, grad_own, grad_far = grads_of(stats, capped_tanh, weight, weight_other)
    mine = got.reshape(half, feature_dim)

    states = jnp.concatenate([mine, lax.ppermute(mine, "c", SWAP)])
    grad_logits = jnp.concatenate([grad_own, lax.ppermute(grad_far, "c", SWAP)])
    head_grad = lax.dot_general(
        states, grad_logits, (((0,), (0,)), ((), ())), preferred_element_type=f32
    )
    grad_head = head_grad.astype(bf16).reshape(head_weight.shape)

    part = sum_pack(lax.all_to_all(part, "x", 0, 0, tiled=True))
    part = lax.all_to_all(part, PLANE, 0, 0, tiled=True)
    grad_hidden = unpacked(jnp.sum(part.astype(f32), axis=0)).astype(bf16)
    return grad_hidden, grad_head


def solution(mesh):
    fine = Mesh(mesh.devices.reshape(tuple(SIZES.values())), tuple(SIZES))
    head = P(None, VOCAB, SEQ, None)
    return jax.shard_map(
        shards,
        mesh=fine,
        in_specs=(P(SEQ, VOCAB), P(SEQ), P(SEQ, VOCAB), head),
        out_specs=(P(SEQ, VOCAB), head),
        check_vma=False,
    )
```

```python
import jax
import jax.numpy as jnp
from jax import lax
from jax.experimental import pallas as pl
from jax.experimental.pallas import tpu as pltpu
from jax.sharding import Mesh
from jax.sharding import PartitionSpec as P

SIZES = {"x": 4, "yh": 2, "c": 2, "yl": 4, "z": 8}
SEQ = ("x", "yh", "c")
VOCAB = ("yl", "z")
PLANE = ("yh", "yl", "z")
SWAP = [(0, 1), (1, 0)]
f32, bf16 = jnp.float32, jnp.bfloat16


KERNEL = pltpu.CompilerParams(vmem_limit_bytes=24 * 1024 * 1024)
IN_HBM = pl.BlockSpec(memory_space=pltpu.HBM)
IN_VMEM = pl.BlockSpec(memory_space=pltpu.VMEM)
HELD = (2, 2304, 256)


def in_hbm(array):
    return pltpu.with_memory_space_constraint(array, pltpu.HBM)


def logits_kernel(
    got_ref,
    own_ref,
    far_ref,
    mass_ref,
    mask_ref,
    far_mask_ref,
    tanh_ref,
    stats_ref,
    held,
    made,
    sems,
    out_sems,
):
    copies = []
    for at in range(2):
        source = far_ref.at[:, pl.ds(256 * at, 256)]
        copies.append(pltpu.make_async_copy(source, held.at[at], sems.at[at]))
        copies[at].start()
    rows = jnp.concatenate([got_ref[at] for at in range(4)], axis=0)
    sums, sent = jnp.zeros((192, 1), f32), []
    for at in range(4):
        columns = slice(256 * at, 256 * at + 256)
        if at >= 2:
            copies[at - 2].wait()
        weight = own_ref[:, columns] if at < 2 else held[at - 2]
        logits = jnp.dot(rows, weight, preferred_element_type=f32)
        capped_tanh = jnp.tanh(logits * (1.0 / 30.0))
        made[at] = capped_tanh
        target = tanh_ref.at[:, pl.ds(256 * at, 256)]
        sent.append(pltpu.make_async_copy(made.at[at], target, out_sems.at[at]))
        sent[at].start()
        sums = sums + jnp.sum(jnp.exp(30.0 * capped_tanh), axis=1, keepdims=True)
    wide = jnp.broadcast_to(sums, (192, 128))
    first = jnp.transpose(wide[:128])[:1]
    last = jnp.concatenate([wide[128:], mass_ref[...], jnp.zeros((40, 128), f32)], axis=0)
    last = jnp.transpose(last)[:1]
    count = jnp.sum(far_mask_ref[...].astype(f32), axis=1, keepdims=True)
    blank, rest = jnp.zeros((1, 88), f32), jnp.zeros((1, 15), f32)
    extra = jnp.concatenate([blank, mask_ref[...].astype(f32), count, rest], axis=1)
    lane = lax.broadcasted_iota(jnp.int32, (1, 128), 1)
    stats = jnp.concatenate([first, jnp.where(lane < 88, last, extra)], axis=0)
    stats_ref[...] = jnp.broadcast_to(stats[None], stats_ref.shape)
    for copy in sent:
        copy.wait()


def logits_of(got, own, far, mass, mask, far_mask):
    wide = pltpu.HBM((192, 1024), f32)
    stats = jax.ShapeDtypeStruct((64, 2, 128), f32)
    return pl.pallas_call(
        logits_kernel,
        in_specs=[IN_VMEM, IN_VMEM, IN_HBM] + [IN_VMEM] * 3,
        out_specs=(IN_HBM, IN_VMEM),
        out_shape=(wide, stats),
        scratch_shapes=[
            pltpu.VMEM(HELD, bf16),
            pltpu.VMEM((4, 192, 256), f32),
            pltpu.SemaphoreType.DMA((2,)),
            pltpu.SemaphoreType.DMA((4,)),
        ],
        compiler_params=KERNEL,
    )(got, own, in_hbm(far), mass, mask, far_mask)


def teacher_kernel(probs_ref, near_ref, give_ref, mass_ref):
    y_at, core = lax.axis_index("yh"), lax.axis_index("c")
    for x_at in range(4):
        for out_ref, y_of in ((near_ref, y_at), (give_ref, 1 - y_at)):
            for which, core_of in enumerate((core, 1 - core)):
                start = pl.multiple_of(2048 * x_at + 1024 * y_of + 512 * core_of, 512)
                out_ref[x_at, :, 512 * which : 512 * which + 512] = probs_ref[:, pl.ds(start, 512)]
    total = probs_ref[:, :128].astype(f32)
    for start in range(128, 8192, 128):
        total = total + probs_ref[:, start : start + 128].astype(f32)
    mass_ref[...] = jnp.broadcast_to(jnp.sum(total, axis=1, keepdims=True), (24, 128))


def teacher_parts(probs):
    part = jax.ShapeDtypeStruct((4, 24, 1024), bf16)
    out = (part, part, jax.ShapeDtypeStruct((24, 128), f32))
    return pl.pallas_call(teacher_kernel, out_shape=out, compiler_params=KERNEL)(probs)


def stats_kernel(stats_ref, target_ref, out_ref):
    first = stats_ref[0, :1, :]
    for at in range(1, 64):
        first = first + stats_ref[at, :1, :]
    halves = []
    for y_at in range(2):
        total = stats_ref[32 * y_at, 1:, :]
        for at in range(1, 32):
            total = total + stats_ref[32 * y_at + at, 1:, :]
        halves.append(total)
    lane = lax.broadcasted_iota(jnp.int32, (1, 128), 1)
    low = jnp.where(lane < 88, halves[0], stats_ref[0, 1:, :])
    high = jnp.where(lane < 88, halves[1], stats_ref[32, 1:, :])
    low = jnp.where(lane < 64, halves[0] + halves[1], low)
    rows = jnp.concatenate([first, low, high, high], axis=0)
    top = rows.astype(bf16).astype(f32)
    middle = (rows - top).astype(bf16).astype(f32)
    split = [top, middle, rows - top - middle, jnp.zeros((36, 128), f32)]
    split = jnp.concatenate(split, axis=0).astype(bf16)
    for at in range(4):
        out_ref[at, :, :1024] = target_ref[at]
        out_ref[at, :, 1024:] = split


def stats_over_plane(stats, target):
    out = jax.ShapeDtypeStruct((4, 48, 1152), bf16)
    return pl.pallas_call(stats_kernel, out_shape=out, compiler_params=KERNEL)(stats, target)


def grads_kernel(
    got_ref,
    tanh_ref,
    own_ref,
    far_ref,
    part_ref,
    grad_own_ref,
    grad_far_ref,
    held,
    made,
    grads,
    sems,
    out_sems,
    grad_sems,
):
    copies = []
    for at in range(6):
        source = (own_ref, far_ref)[at % 2].at[pl.ds(768 * (at // 2), 768), :]
        copies.append(pltpu.make_async_copy(source, held.at[at], sems.at[at]))
        copies[at].start()
    stats = []
    for at in range(4):
        split = got_ref[at, :, 1024:].astype(f32)
        stats.append(split[0:4] + split[4:8] + split[8:12])
    firsts = [stats[at][:1] for at in range(4)]
    seconds = [stats[at // 2][1 + at % 2 : 2 + at % 2] for at in range(8)]
    rows = jnp.concatenate([sum(firsts), sum(seconds[::2])] + seconds, axis=0)
    lane = lax.broadcasted_iota(jnp.int32, (1, 128), 1)
    counted = jnp.where((lane >= 88) & (lane < 113), sum(seconds), 0.0)
    factor = 8.0 * 262144 / jnp.sum(counted, axis=1, keepdims=True)
    columns = jnp.transpose(jnp.concatenate([rows, jnp.zeros((118, 128), f32)], axis=0))
    sum_exp = jnp.concatenate([columns[:, 0:1], columns[:64, 1:2]], axis=0)
    mass = jnp.concatenate([columns[64:88, 2 + at : 3 + at] for at in range(8)], axis=0)
    mask = jnp.concatenate([columns[88:112, 2 + at : 3 + at] for at in range(8)], axis=0)
    scale, share = factor * mask, mass / sum_exp
    sent = []
    for at, grad_ref in enumerate((grad_own_ref, grad_far_ref)):
        entries = slice(512 * at, 512 * at + 512)
        capped_tanh = tanh_ref[:, entries]
        target = jnp.concatenate([got_ref[x_at, :, entries].astype(f32) for x_at in range(4)])
        grad = jnp.exp(30.0 * capped_tanh) * share - target
        grads[at] = (scale * grad * (1.0 - capped_tanh * capped_tanh)).astype(bf16)
        sent.append(pltpu.make_async_copy(grads.at[at], grad_ref, grad_sems.at[at]))
        sent[at].start()
    dims = (((1,), (1,)), ((), ()))
    for at in range(3):
        copies[2 * at].wait()
        copies[2 * at + 1].wait()
        for start in (0, 384):
            inner = slice(start, start + 384)
            part = lax.dot_general(
                grads[0], held[2 * at, inner, :], dims, preferred_element_type=f32
            ) + lax.dot_general(
                grads[1], held[2 * at + 1, inner, :], dims, preferred_element_type=f32
            )
            part = part.astype(bf16)
            for x_at in range(4):
                made[at, x_at, :, inner] = part[48 * x_at : 48 * x_at + 48]
        target = part_ref.at[:, :, pl.ds(768 * at, 768)]
        sent.append(pltpu.make_async_copy(made.at[at], target, out_sems.at[at]))
        sent[2 + at].start()
    for copy in sent:
        copy.wait()


def grads_of(got, capped_tanh, own, far):
    grad = pltpu.HBM((192, 512), bf16)
    return pl.pallas_call(
        grads_kernel,
        in_specs=[IN_VMEM] * 2 + [IN_HBM] * 2,
        out_specs=(IN_HBM, IN_HBM, IN_HBM),
        out_shape=(pltpu.HBM((4, 48, own.shape[0]), bf16), grad, grad),
        scratch_shapes=[
            pltpu.VMEM((6, 768, 512), bf16),
            pltpu.VMEM((3, 4, 48, 768), bf16),
            pltpu.VMEM((2, 192, 512), bf16),
            pltpu.SemaphoreType.DMA((6,)),
            pltpu.SemaphoreType.DMA((3,)),
            pltpu.SemaphoreType.DMA((2,)),
        ],
        compiler_params=KERNEL,
    )(got, capped_tanh, in_hbm(own), in_hbm(far))


def packed(block):
    first, second, third = block[:8], block[8:16], block[16:]
    top = jnp.concatenate([first, second[:, :56]], axis=1)
    rest = jnp.concatenate([second[:, 56:], third, jnp.zeros((8, 40), block.dtype)], axis=1)
    return jnp.concatenate([top, rest], axis=0)


def unpacked(block):
    top, rest = block[..., :8, :], block[..., 8:, :]
    second = jnp.concatenate([top[..., 72:], rest[..., :16]], axis=-1)
    return jnp.concatenate([top[..., :72], second, rest[..., 16:88]], axis=-2)


def pack_copies_kernel(block_ref, out_ref):
    block = packed(block_ref[...].astype(f32)).astype(bf16)
    out_ref[...] = jnp.broadcast_to(block[None], out_ref.shape)


def pack_copies(block):
    out = jax.ShapeDtypeStruct((64, 16, 128), bf16)
    return pl.pallas_call(pack_copies_kernel, out_shape=out)(block)


def unpack_rows_kernel(plane_ref, out_ref):
    rows = [
        jnp.concatenate(
            [unpacked(plane_ref[32 * y_at + shard].astype(f32)) for shard in range(32)], axis=1
        )
        for y_at in range(2)
    ]
    out_ref[...] = jnp.concatenate(rows, axis=0).astype(bf16)


def unpack_rows(plane):
    out = jax.ShapeDtypeStruct((48, 2304), bf16)
    return pl.pallas_call(unpack_rows_kernel, out_shape=out, compiler_params=KERNEL)(plane)


def sum_pack_kernel(parts_ref, out_ref, held, sems):
    copies = []
    for at in range(2):
        source = parts_ref.at[:, :, pl.ds(1152 * at, 1152)]
        copies.append(pltpu.make_async_copy(source, held.at[at], sems.at[at]))
        copies[at].start()
    for at in range(2):
        copies[at].wait()
        total = held[at, 0].astype(f32)
        for x_at in range(1, 4):
            total = total + held[at, x_at].astype(f32)
        for shard in range(16):
            columns = total[:, 72 * shard : 72 * shard + 72]
            for y_at in range(2):
                block = packed(columns[24 * y_at : 24 * y_at + 24])
                out_ref[32 * y_at + 16 * at + shard] = block.astype(bf16)


def sum_pack(parts):
    return pl.pallas_call(
        sum_pack_kernel,
        in_specs=[IN_HBM],
        out_shape=jax.ShapeDtypeStruct((64, 16, 128), bf16),
        scratch_shapes=[pltpu.VMEM((2, 4, 48, 1152), bf16), pltpu.SemaphoreType.DMA((2,))],
        compiler_params=KERNEL,
    )(parts)


def shards(hidden_states, loss_mask, teacher_probs, head_weight):
    tokens, features = hidden_states.shape
    feature_dim, shard_cols = head_weight.shape[0], head_weight.shape[3]
    half = 8 * tokens
    weight = head_weight.reshape(feature_dim, shard_cols)
    y_at = lax.axis_index("yh")

    copies, weight, teacher_probs, loss_mask = lax.optimization_barrier(
        (pack_copies(hidden_states), weight, teacher_probs, loss_mask)
    )
    rows = unpack_rows(lax.all_to_all(copies, PLANE, 0, 0, tiled=True))

    weight_other = lax.ppermute(weight, "c", SWAP)
    mask_other = lax.ppermute(loss_mask, "c", SWAP)

    near, give, mass_part = teacher_parts(teacher_probs)
    came = lax.ppermute(give, "yh", SWAP)

    rows, mask_other = lax.optimization_barrier((rows, mask_other))
    got = lax.all_gather(rows, "x", axis=0)
    got, came = lax.optimization_barrier((got, came))
    low, high = jnp.where(y_at == 0, near, came), jnp.where(y_at == 0, came, near)
    target = jnp.concatenate([low, high], axis=1)

    capped_tanh, stats = logits_of(
        got, weight, weight_other, mass_part, loss_mask[None], mask_other[None]
    )
    stats = stats_over_plane(lax.all_to_all(stats, PLANE, 0, 0, tiled=True), target)
    stats = lax.all_to_all(stats, "x", 0, 0, tiled=True)
    part, grad_own, grad_far = grads_of(stats, capped_tanh, weight, weight_other)
    mine = got.reshape(half, feature_dim)

    states = jnp.concatenate([mine, lax.ppermute(mine, "c", SWAP)])
    grad_logits = jnp.concatenate([grad_own, lax.ppermute(grad_far, "c", SWAP)])
    head_grad = lax.dot_general(
        states, grad_logits, (((0,), (0,)), ((), ())), preferred_element_type=f32
    )
    grad_head = head_grad.astype(bf16).reshape(head_weight.shape)

    part = sum_pack(lax.all_to_all(part, "x", 0, 0, tiled=True))
    part = lax.all_to_all(part, PLANE, 0, 0, tiled=True)
    grad_hidden = unpacked(jnp.sum(part.astype(f32), axis=0)).astype(bf16)
    return grad_hidden, grad_head


def solution(mesh):
    fine = Mesh(mesh.devices.reshape(tuple(SIZES.values())), tuple(SIZES))
    head = P(None, VOCAB, SEQ, None)
    return jax.shard_map(
        shards,
        mesh=fine,
        in_specs=(P(SEQ, VOCAB), P(SEQ), P(SEQ, VOCAB), head),
        out_specs=(P(SEQ, VOCAB), head),
        check_vma=False,
    )
```

```python
import jax
import jax.numpy as jnp
from jax import lax
from jax.experimental import pallas as pl
from jax.experimental.pallas import tpu as pltpu
from jax.sharding import Mesh
from jax.sharding import PartitionSpec as P

SIZES = {"x": 4, "yh": 2, "c": 2, "yl": 4, "z": 8}
SEQ = ("x", "yh", "c")
VOCAB = ("yl", "z")
PLANE = ("yh", "yl", "z")
SWAP = [(0, 1), (1, 0)]
f32, bf16 = jnp.float32, jnp.bfloat16


KERNEL = pltpu.CompilerParams(vmem_limit_bytes=24 * 1024 * 1024)
IN_HBM = pl.BlockSpec(memory_space=pltpu.HBM)
IN_VMEM = pl.BlockSpec(memory_space=pltpu.VMEM)
HELD = (2, 2304, 256)


def in_hbm(array):
    return pltpu.with_memory_space_constraint(array, pltpu.HBM)


def logits_kernel(
    got_ref,
    own_ref,
    far_ref,
    mass_ref,
    mask_ref,
    far_mask_ref,
    tanh_ref,
    stats_ref,
    held,
    made,
    sems,
    out_sems,
):
    copies = []
    for at in range(2):
        source = far_ref.at[:, pl.ds(256 * at, 256)]
        copies.append(pltpu.make_async_copy(source, held.at[at], sems.at[at]))
        copies[at].start()
    rows = jnp.concatenate([got_ref[at] for at in range(4)], axis=0)
    sums, sent = jnp.zeros((192, 1), f32), []
    for at in range(4):
        columns = slice(256 * at, 256 * at + 256)
        if at >= 2:
            copies[at - 2].wait()
        weight = own_ref[:, columns] if at < 2 else held[at - 2]
        logits = jnp.dot(rows, weight, preferred_element_type=f32)
        capped_tanh = jnp.tanh(logits * (1.0 / 30.0))
        made[at] = capped_tanh
        target = tanh_ref.at[:, pl.ds(256 * at, 256)]
        sent.append(pltpu.make_async_copy(made.at[at], target, out_sems.at[at]))
        sent[at].start()
        sums = sums + jnp.sum(jnp.exp(30.0 * capped_tanh), axis=1, keepdims=True)
    wide = jnp.broadcast_to(sums, (192, 128))
    first = jnp.transpose(wide[:128])[:1]
    last = jnp.concatenate([wide[128:], mass_ref[...], jnp.zeros((40, 128), f32)], axis=0)
    last = jnp.transpose(last)[:1]
    count = jnp.sum(far_mask_ref[...].astype(f32), axis=1, keepdims=True)
    blank, rest = jnp.zeros((1, 88), f32), jnp.zeros((1, 15), f32)
    extra = jnp.concatenate([blank, mask_ref[...].astype(f32), count, rest], axis=1)
    lane = lax.broadcasted_iota(jnp.int32, (1, 128), 1)
    stats = jnp.concatenate([first, jnp.where(lane < 88, last, extra)], axis=0)
    stats_ref[...] = jnp.broadcast_to(stats[None], stats_ref.shape)
    for copy in sent:
        copy.wait()


def logits_of(got, own, far, mass, mask, far_mask):
    wide = pltpu.HBM((192, 1024), f32)
    stats = jax.ShapeDtypeStruct((64, 2, 128), f32)
    return pl.pallas_call(
        logits_kernel,
        in_specs=[IN_VMEM, IN_VMEM, IN_HBM] + [IN_VMEM] * 3,
        out_specs=(IN_HBM, IN_VMEM),
        out_shape=(wide, stats),
        scratch_shapes=[
            pltpu.VMEM(HELD, bf16),
            pltpu.VMEM((4, 192, 256), f32),
            pltpu.SemaphoreType.DMA((2,)),
            pltpu.SemaphoreType.DMA((4,)),
        ],
        compiler_params=KERNEL,
    )(got, own, in_hbm(far), mass, mask, far_mask)


def teacher_kernel(probs_ref, near_ref, give_ref, mass_ref):
    y_at, core = lax.axis_index("yh"), lax.axis_index("c")
    for x_at in range(4):
        for out_ref, y_of in ((near_ref, y_at), (give_ref, 1 - y_at)):
            for which, core_of in enumerate((core, 1 - core)):
                start = pl.multiple_of(2048 * x_at + 1024 * y_of + 512 * core_of, 512)
                out_ref[x_at, :, 512 * which : 512 * which + 512] = probs_ref[:, pl.ds(start, 512)]
    total = probs_ref[:, :128].astype(f32)
    for start in range(128, 8192, 128):
        total = total + probs_ref[:, start : start + 128].astype(f32)
    mass_ref[...] = jnp.broadcast_to(jnp.sum(total, axis=1, keepdims=True), (24, 128))


def teacher_parts(probs):
    part = jax.ShapeDtypeStruct((4, 24, 1024), bf16)
    out = (part, part, jax.ShapeDtypeStruct((24, 128), f32))
    return pl.pallas_call(teacher_kernel, out_shape=out, compiler_params=KERNEL)(probs)


def stats_kernel(stats_ref, target_ref, out_ref):
    first = stats_ref[0, :1, :]
    for at in range(1, 64):
        first = first + stats_ref[at, :1, :]
    halves = []
    for y_at in range(2):
        total = stats_ref[32 * y_at, 1:, :]
        for at in range(1, 32):
            total = total + stats_ref[32 * y_at + at, 1:, :]
        halves.append(total)
    lane = lax.broadcasted_iota(jnp.int32, (1, 128), 1)
    low = jnp.where(lane < 88, halves[0], stats_ref[0, 1:, :])
    high = jnp.where(lane < 88, halves[1], stats_ref[32, 1:, :])
    low = jnp.where(lane < 64, halves[0] + halves[1], low)
    rows = jnp.concatenate([first, low, high, high], axis=0)
    top = rows.astype(bf16).astype(f32)
    middle = (rows - top).astype(bf16).astype(f32)
    split = [top, middle, rows - top - middle, jnp.zeros((36, 128), f32)]
    split = jnp.concatenate(split, axis=0).astype(bf16)
    for at in range(4):
        out_ref[at, :, :1024] = target_ref[at]
        out_ref[at, :, 1024:] = split


def stats_over_plane(stats, target):
    out = jax.ShapeDtypeStruct((4, 48, 1152), bf16)
    return pl.pallas_call(stats_kernel, out_shape=out, compiler_params=KERNEL)(stats, target)


def grads_kernel(
    got_ref,
    tanh_ref,
    own_ref,
    far_ref,
    part_ref,
    grad_own_ref,
    grad_far_ref,
    held,
    made,
    grads,
    sems,
    out_sems,
    grad_sems,
):
    copies = []
    for at in range(6):
        source = (own_ref, far_ref)[at % 2].at[pl.ds(768 * (at // 2), 768), :]
        copies.append(pltpu.make_async_copy(source, held.at[at], sems.at[at]))
        copies[at].start()
    stats = []
    for at in range(4):
        split = got_ref[at, :, 1024:].astype(f32)
        stats.append(split[0:4] + split[4:8] + split[8:12])
    firsts = [stats[at][:1] for at in range(4)]
    seconds = [stats[at // 2][1 + at % 2 : 2 + at % 2] for at in range(8)]
    rows = jnp.concatenate([sum(firsts), sum(seconds[::2])] + seconds, axis=0)
    lane = lax.broadcasted_iota(jnp.int32, (1, 128), 1)
    counted = jnp.where((lane >= 88) & (lane < 113), sum(seconds), 0.0)
    factor = 8.0 * 262144 / jnp.sum(counted, axis=1, keepdims=True)
    columns = jnp.transpose(jnp.concatenate([rows, jnp.zeros((118, 128), f32)], axis=0))
    sum_exp = jnp.concatenate([columns[:, 0:1], columns[:64, 1:2]], axis=0)
    mass = jnp.concatenate([columns[64:88, 2 + at : 3 + at] for at in range(8)], axis=0)
    mask = jnp.concatenate([columns[88:112, 2 + at : 3 + at] for at in range(8)], axis=0)
    scale, share = factor * mask, mass / sum_exp
    sent = []
    for at, grad_ref in enumerate((grad_own_ref, grad_far_ref)):
        entries = slice(512 * at, 512 * at + 512)
        capped_tanh = tanh_ref[:, entries]
        target = jnp.concatenate([got_ref[x_at, :, entries].astype(f32) for x_at in range(4)])
        grad = jnp.exp(30.0 * capped_tanh) * share - target
        grads[at] = (scale * grad * (1.0 - capped_tanh * capped_tanh)).astype(bf16)
        sent.append(pltpu.make_async_copy(grads.at[at], grad_ref, grad_sems.at[at]))
        sent[at].start()
    dims = (((1,), (1,)), ((), ()))
    for at in range(3):
        copies[2 * at].wait()
        copies[2 * at + 1].wait()
        for start in (0, 384):
            inner = slice(start, start + 384)
            part = lax.dot_general(
                grads[0], held[2 * at, inner, :], dims, preferred_element_type=f32
            ) + lax.dot_general(
                grads[1], held[2 * at + 1, inner, :], dims, preferred_element_type=f32
            )
            part = part.astype(bf16)
            for x_at in range(4):
                made[at, x_at, :, inner] = part[48 * x_at : 48 * x_at + 48]
        target = part_ref.at[:, :, pl.ds(768 * at, 768)]
        sent.append(pltpu.make_async_copy(made.at[at], target, out_sems.at[at]))
        sent[2 + at].start()
    for copy in sent:
        copy.wait()


def grads_of(got, capped_tanh, own, far):
    grad = pltpu.HBM((192, 512), bf16)
    return pl.pallas_call(
        grads_kernel,
        in_specs=[IN_VMEM] * 2 + [IN_HBM] * 2,
        out_specs=(IN_HBM, IN_HBM, IN_HBM),
        out_shape=(pltpu.HBM((4, 48, own.shape[0]), bf16), grad, grad),
        scratch_shapes=[
            pltpu.VMEM((6, 768, 512), bf16),
            pltpu.VMEM((3, 4, 48, 768), bf16),
            pltpu.VMEM((2, 192, 512), bf16),
            pltpu.SemaphoreType.DMA((6,)),
            pltpu.SemaphoreType.DMA((3,)),
            pltpu.SemaphoreType.DMA((2,)),
        ],
        compiler_params=KERNEL,
    )(got, capped_tanh, in_hbm(own), in_hbm(far))


def packed(block):
    first, second, third = block[:8], block[8:16], block[16:]
    top = jnp.concatenate([first, second[:, :56]], axis=1)
    rest = jnp.concatenate([second[:, 56:], third, jnp.zeros((8, 40), block.dtype)], axis=1)
    return jnp.concatenate([top, rest], axis=0)


def unpacked(block):
    top, rest = block[..., :8, :], block[..., 8:, :]
    second = jnp.concatenate([top[..., 72:], rest[..., :16]], axis=-1)
    return jnp.concatenate([top[..., :72], second, rest[..., 16:88]], axis=-2)


def pack_copies_kernel(block_ref, out_ref):
    block = packed(block_ref[...].astype(f32)).astype(bf16)
    out_ref[...] = jnp.broadcast_to(block[None], out_ref.shape)


def pack_copies(block):
    out = jax.ShapeDtypeStruct((64, 16, 128), bf16)
    return pl.pallas_call(pack_copies_kernel, out_shape=out)(block)


def unpack_rows_kernel(plane_ref, out_ref):
    rows = [
        jnp.concatenate(
            [unpacked(plane_ref[32 * y_at + shard].astype(f32)) for shard in range(32)], axis=1
        )
        for y_at in range(2)
    ]
    out_ref[...] = jnp.concatenate(rows, axis=0).astype(bf16)


def unpack_rows(plane):
    out = jax.ShapeDtypeStruct((48, 2304), bf16)
    return pl.pallas_call(unpack_rows_kernel, out_shape=out, compiler_params=KERNEL)(plane)


def sum_unpack_kernel(parts_ref, out_ref):
    totals = []
    for start in range(0, 64, 16):
        total = parts_ref[start].astype(f32)
        for at in range(start + 1, start + 16):
            total = total + parts_ref[at].astype(f32)
        totals.append(total)
    out_ref[...] = unpacked(sum(totals)).astype(bf16)


def sum_unpack(parts):
    out = jax.ShapeDtypeStruct((24, 72), bf16)
    return pl.pallas_call(sum_unpack_kernel, out_shape=out, compiler_params=KERNEL)(parts)


def sum_pack_kernel(parts_ref, out_ref, held, sems):
    copies = []
    for at in range(2):
        source = parts_ref.at[:, :, pl.ds(1152 * at, 1152)]
        copies.append(pltpu.make_async_copy(source, held.at[at], sems.at[at]))
        copies[at].start()
    for at in range(2):
        copies[at].wait()
        total = held[at, 0].astype(f32)
        for x_at in range(1, 4):
            total = total + held[at, x_at].astype(f32)
        for shard in range(16):
            columns = total[:, 72 * shard : 72 * shard + 72]
            for y_at in range(2):
                block = packed(columns[24 * y_at : 24 * y_at + 24])
                out_ref[32 * y_at + 16 * at + shard] = block.astype(bf16)


def sum_pack(parts):
    return pl.pallas_call(
        sum_pack_kernel,
        in_specs=[IN_HBM],
        out_shape=jax.ShapeDtypeStruct((64, 16, 128), bf16),
        scratch_shapes=[pltpu.VMEM((2, 4, 48, 1152), bf16), pltpu.SemaphoreType.DMA((2,))],
        compiler_params=KERNEL,
    )(parts)


def shards(hidden_states, loss_mask, teacher_probs, head_weight):
    tokens, features = hidden_states.shape
    feature_dim, shard_cols = head_weight.shape[0], head_weight.shape[3]
    half = 8 * tokens
    weight = head_weight.reshape(feature_dim, shard_cols)
    y_at = lax.axis_index("yh")

    copies, weight, teacher_probs, loss_mask = lax.optimization_barrier(
        (pack_copies(hidden_states), weight, teacher_probs, loss_mask)
    )
    rows = unpack_rows(lax.all_to_all(copies, PLANE, 0, 0, tiled=True))

    weight_other = lax.ppermute(weight, "c", SWAP)
    mask_other = lax.ppermute(loss_mask, "c", SWAP)

    near, give, mass_part = teacher_parts(teacher_probs)
    came = lax.ppermute(give, "yh", SWAP)

    rows, mask_other = lax.optimization_barrier((rows, mask_other))
    got = lax.all_gather(rows, "x", axis=0)
    got, came = lax.optimization_barrier((got, came))
    low, high = jnp.where(y_at == 0, near, came), jnp.where(y_at == 0, came, near)
    target = jnp.concatenate([low, high], axis=1)

    capped_tanh, stats = logits_of(
        got, weight, weight_other, mass_part, loss_mask[None], mask_other[None]
    )
    stats = stats_over_plane(lax.all_to_all(stats, PLANE, 0, 0, tiled=True), target)
    stats = lax.all_to_all(stats, "x", 0, 0, tiled=True)
    part, grad_own, grad_far = grads_of(stats, capped_tanh, weight, weight_other)
    mine = got.reshape(half, feature_dim)

    states = jnp.concatenate([mine, lax.ppermute(mine, "c", SWAP)])
    grad_logits = jnp.concatenate([grad_own, lax.ppermute(grad_far, "c", SWAP)])
    head_grad = lax.dot_general(
        states, grad_logits, (((0,), (0,)), ((), ())), preferred_element_type=f32
    )
    grad_head = head_grad.astype(bf16).reshape(head_weight.shape)

    part = sum_pack(lax.all_to_all(part, "x", 0, 0, tiled=True))
    grad_hidden = sum_unpack(lax.all_to_all(part, PLANE, 0, 0, tiled=True))
    return grad_hidden, grad_head


def solution(mesh):
    fine = Mesh(mesh.devices.reshape(tuple(SIZES.values())), tuple(SIZES))
    head = P(None, VOCAB, SEQ, None)
    return jax.shard_map(
        shards,
        mesh=fine,
        in_specs=(P(SEQ, VOCAB), P(SEQ), P(SEQ, VOCAB), head),
        out_specs=(P(SEQ, VOCAB), head),
        check_vma=False,
    )
```
